256 devices in a mesh: row: 8 (over y, core), col: 8 (over z), dp: 4 (over x).
Axes of the slice: x: 4, y: 4, z: 8, core: 2. Of those that a mesh axis runs over, the one named last changes fastest.
Arguments:
- acts: bfloat16 [2048, 8192], P('dp', 'row'), may hold values from -6 to 6
- cot_hidden: bfloat16 [2048, 15360], P(('dp', 'row'), 'col'), may hold values from -6 to 6
- gate_pre: bfloat16 [2048, 15360], P(('dp', 'row'), 'col'), may hold values from -6 to 6
- up_pre: bfloat16 [2048, 15360], P(('dp', 'row'), 'col'), may hold values from -6 to 6
- w_gate: bfloat16 [8192, 15360], P('row', 'col'), may hold values from -0.0625 to 0.0625
- w_up: bfloat16 [8192, 15360], P('row', 'col'), may hold values from -0.0625 to 0.0625
- gate_down_factor: bfloat16 [8192, 64], replicated, may hold values from -0.0625 to 0.0625
- up_down_factor: bfloat16 [8192, 64], replicated, may hold values from -0.0625 to 0.0625
- b_gate: bfloat16 [64, 15360], P(None, 'col'), may hold values from -0.09375 to 0.09375
- b_up: bfloat16 [64, 15360], P(None, 'col'), may hold values from -0.09375 to 0.09375
Outputs:
- normed_input_gradient: bfloat16 [2048, 8192], P(('dp', 'col'), 'row')
- grad_a_gate: float32 [8192, 64], P(('row', 'col', 'dp'))
- grad_a_up: float32 [8192, 64], P(('row', 'col', 'dp'))
- grad_b_gate: float32 [64, 15360], P(None, ('col', 'row', 'dp'))
- grad_b_up: float32 [64, 15360], P(None, ('col', 'row', 'dp'))
The draws below stay inside these ranges and needn't reach their ends.
All inputs are finite; a program needn't handle non-finite values.
Results may differ from the reference program's by a relative error of at most 0.012.
Values may be sent and summed in bfloat16 or wider, within the bound.
A program may use at most 64 MiB of HBM per device.

```python
import jax
import jax.numpy as jnp

D = 8192
FF = 15360
RANK = 64
TOKENS = 2048


def raised(result, own_key, source, target, shards_of, factor):
    owner, partner = [(jnp.arange(result.shape[dim]) // (result.shape[dim] // shards_of)).reshape([-1 if axis == dim else 1 for axis in range(result.ndim)]) for dim in (source, target)]
    chosen = jax.random.permutation(own_key, shards_of)[partner]
    strong = (owner == chosen) | (owner == (partner + shards_of // 2) % shards_of)
    return jnp.where(strong, factor * result, result)


def levels(rng, dims, split, least, top_value):
    factor_of, own = 1.0, jax.random.fold_in(rng, 6)
    for position, parts in split:
        steps = jnp.exp(jax.random.uniform(jax.random.fold_in(own, position), (parts,), jnp.float32, least / len(split), top_value / len(split)))
        factor_of = factor_of * jnp.repeat(steps, dims[position] // parts).reshape([-1 if axis == position else 1 for axis in range(len(dims))])
    return factor_of


def gaussian(key, dims, spread, reach, cuts=(), held_as=jnp.bfloat16):
    array = jax.random.normal(key, dims, jnp.float32) * spread
    if len(cuts) > 0:
        array = levels(key, dims, cuts, -0.22, 0.18) * array
    return jnp.clip(array, min=-reach, max=reach).astype(held_as)


def gaussian_with(own_key, shape, width, most, split, heavy, dtype=jnp.bfloat16):
    result = width * jax.random.normal(own_key, shape, jnp.float32)
    if split:
        result = result * levels(own_key, shape, split, -0.22, 0.18)
    return jnp.clip(raised(result, jax.random.fold_in(own_key, 3), *heavy), -most, most).astype(dtype)


def setup_inputs(seed: int = 0) -> dict:
    streams_of = jax.random.split(jax.random.key(seed), 11)
    return {
        "acts": gaussian(streams_of[0], (TOKENS, D), 1.0, 6.0, ((0, 4), (1, 8))),
        "cot_hidden": gaussian_with(streams_of[1], (TOKENS, FF), 1.0, 6.0, ((0, 32), (1, 8)), (0, 1, 32, 2.75)),
        "gate_pre": gaussian(streams_of[2], (TOKENS, FF), 1.0, 6.0, ((0, 32), (1, 8))),
        "up_pre": gaussian(streams_of[3], (TOKENS, FF), 1.0, 6.0, ((0, 32), (1, 8))),
        "w_gate": gaussian(streams_of[4], (D, FF), D ** -0.5, 0.0625, ((0, 8), (1, 8))),
        "w_up": gaussian(streams_of[5], (D, FF), D ** -0.5, 0.0625, ((0, 8), (1, 8))),
        "gate_down_factor": gaussian(streams_of[6], (D, RANK), D ** -0.5, 0.0625),
        "up_down_factor": gaussian(streams_of[7], (D, RANK), D ** -0.5, 0.0625),
        "b_gate": gaussian(streams_of[8], (RANK, FF), (FF // 4) ** -0.5, 0.09375, ((1, 8),)),
        "b_up": gaussian(streams_of[9], (RANK, FF), (FF // 4) ** -0.5, 0.09375, ((1, 8),)),
    }


def gated_back(cot_hidden, gate_pre, up_pre):
    gate_f = gate_pre.astype(jnp.float32)
    sig = jax.nn.sigmoid(gate_f)
    hid = cot_hidden.astype(jnp.float32)
    d_gate = (hid * up_pre.astype(jnp.float32) * sig * (1.0 + gate_f * (1.0 - sig))).astype(jnp.bfloat16)
    d_up = (hid * gate_f * sig).astype(jnp.bfloat16)
    return d_gate, d_up


def reference(acts, cot_hidden, gate_pre, up_pre, w_gate, w_up, gate_down_factor, up_down_factor, b_gate, b_up):
    d_gate, d_up = gated_back(cot_hidden, gate_pre, up_pre)
    gate_rank_projection = jnp.dot(d_gate, b_gate.T, preferred_element_type=jnp.float32).astype(jnp.bfloat16)
    up_rank_projection = jnp.dot(d_up, b_up.T, preferred_element_type=jnp.float32).astype(jnp.bfloat16)
    low_gate = jnp.dot(acts, gate_down_factor, preferred_element_type=jnp.float32).astype(jnp.bfloat16)
    low_up = jnp.dot(acts, up_down_factor, preferred_element_type=jnp.float32).astype(jnp.bfloat16)
    frozen_term = jnp.dot(d_gate, w_gate.T, preferred_element_type=jnp.float32)
    frozen_term = frozen_term + jnp.dot(d_up, w_up.T, preferred_element_type=jnp.float32)
    adapter_term = jnp.dot(gate_rank_projection, gate_down_factor.T, preferred_element_type=jnp.float32)
    adapter_term = adapter_term + jnp.dot(up_rank_projection, up_down_factor.T, preferred_element_type=jnp.float32)
    normed_input_gradient = (frozen_term + 2.0 * adapter_term).astype(jnp.bfloat16)
    factor = 2.0 / TOKENS
    grad_a_gate = factor * jnp.dot(acts.T, gate_rank_projection, preferred_element_type=jnp.float32)
    grad_a_up = factor * jnp.dot(acts.T, up_rank_projection, preferred_element_type=jnp.float32)
    grad_b_gate = factor * jnp.dot(low_gate.T, d_gate, preferred_element_type=jnp.float32)
    grad_b_up = factor * jnp.dot(low_up.T, d_up, preferred_element_type=jnp.float32)
    return normed_input_gradient, grad_a_gate, grad_a_up, grad_b_gate, grad_b_up
```

```python
import jax
import jax.numpy as jnp
from jax import lax
from jax.experimental import pallas as pl
from jax.experimental.pallas import tpu as pltpu
from jax.sharding import PartitionSpec as P

MESH = pl.DeviceIdType.MESH
F32, BF16 = jnp.float32, jnp.bfloat16
ADAPTER_SCALE = 2.0
NY, NZ, NX = 4, 8, 4
ROWS = 2 * NY
CHUNK = 16


def times_transposed(left, right):
    return lax.dot_general(
        left, right, (((1,), (1,)), ((), ())), preferred_element_type=F32
    )


def kernel(
    acts,
    cot,
    gate_pre,
    up_pre,
    w_gate,
    w_up,
    gate_factor,
    up_factor,
    b_gate,
    b_up,
    out,
    ga_gate,
    ga_up,
    gb_gate,
    gb_up,
    pre,
    w,
    b,
    fac,
    act_rows,
    act_cols,
    d,
    part,
    first,
    zm,
    zp,
    adapter,
    rank_part,
    rank_all,
    low_part,
    low_piece,
    low_sum,
    low_all,
    ga_send,
    ga_recv,
    gb_send,
    gb_recv,
    in_sem,
    y_send,
    y_recv,
    p_send,
    p_recv,
    z_send,
    z_recv,
    rz_send,
    rz_recv,
    ry_send,
    ry_recv,
    rp_send,
    rp_recv,
    ls_send,
    ls_recv,
    lg_send,
    lg_recv,
    lz_send,
    lz_recv,
    ga_ssem,
    ga_rsem,
    gb_ssem,
    gb_rsem,
):
    own_tok, hid = cot.shape
    group_tok, width = acts.shape
    n_chunk = own_tok // CHUNK
    factor = 2.0 / (group_tok * NX)
    r, c, x = lax.axis_index("row"), lax.axis_index("col"), lax.axis_index("dp")
    y, core = r // 2, r % 2

    def row_of(step):
        return ((y + step) % NY) * 2 + core

    right, left, far = row_of(1), row_of(NY - 1), row_of(2)
    partner = y * 2 + (1 - core)

    width_at = pl.multiple_of(r * width, width)
    sub = width // NZ
    loads = [
        pltpu.make_async_copy(cot, pre.at[0], in_sem.at[0]),
        pltpu.make_async_copy(gate_pre, pre.at[1], in_sem.at[1]),
        pltpu.make_async_copy(up_pre, pre.at[2], in_sem.at[2]),
        pltpu.make_async_copy(b_gate, b.at[0:64, 0:hid], in_sem.at[3]),
        pltpu.make_async_copy(b_up, b.at[64:128, hid : 2 * hid], in_sem.at[4]),
        pltpu.make_async_copy(
            acts.at[pl.ds(pl.multiple_of(c * own_tok, own_tok), own_tok), :], act_rows, in_sem.at[5]
        ),
        pltpu.make_async_copy(
            gate_factor.at[:, pl.ds(width_at, width)], fac.at[0:64], in_sem.at[6]
        ),
        pltpu.make_async_copy(
            up_factor.at[:, pl.ds(width_at, width)], fac.at[64:128], in_sem.at[7]
        ),
        pltpu.make_async_copy(
            acts.at[:, pl.ds(pl.multiple_of(c * sub, sub), sub)], act_cols, in_sem.at[8]
        ),
        pltpu.make_async_copy(w_gate, w.at[:, 0:hid], in_sem.at[9]),
        pltpu.make_async_copy(w_up, w.at[:, hid : 2 * hid], in_sem.at[10]),
    ]
    for load in loads:
        load.start()

    barrier = pltpu.get_barrier_semaphore()
    for step in range(1, ROWS):
        pl.semaphore_signal(barrier, 1, device_id={"row": (r + step) % ROWS}, device_id_type=MESH)
    for step in range(1, NZ):
        pl.semaphore_signal(barrier, 1, device_id={"col": (c + step) % NZ}, device_id_type=MESH)
    for step in range(1, NX):
        pl.semaphore_signal(barrier, 1, device_id={"dp": (x + step) % NX}, device_id_type=MESH)

    sent = []

    def remote(src, dst, ssem, rsem, **where):
        return pltpu.make_async_remote_copy(
            src_ref=src,
            dst_ref=dst,
            send_sem=ssem,
            recv_sem=rsem,
            device_id=where,
            device_id_type=MESH,
        )

    def start(copy):
        copy.start()
        sent.append(copy)

    def cotangents(q):
        rows = slice(q * CHUNK, (q + 1) * CHUNK)
        gate = pre[1, rows, :].astype(F32)
        sig = jax.nn.sigmoid(gate)
        hot = pre[0, rows, :].astype(F32)
        up = pre[2, rows, :].astype(F32)
        d[q, r, :, 0:hid] = (hot * up * sig * (1.0 + gate * (1.0 - sig))).astype(BF16)
        d[q, r, :, hid : 2 * hid] = (hot * gate * sig).astype(BF16)

    def y_copy(q, kind):
        if kind == 0:
            ref, to = d.at[q, r], right
        elif kind == 1:
            ref, to = d.at[q, r], left
        elif kind == 2:
            ref, to = d.at[q, left, :, 0:hid], right
        else:
            ref, to = d.at[q, right, :, hid : 2 * hid], left
        return remote(ref, ref, y_send.at[q, kind], y_recv.at[q, kind], row=to)

    def p_copy(q, kind):
        ref = d.at[q, (r, left, right, far)[kind]]
        return remote(ref, ref, p_send.at[q, kind], p_recv.at[q, kind], row=partner)

    def own(q):
        start(y_copy(q, 0))
        start(y_copy(q, 1))

    def near(q):
        y_copy(q, 0).wait_recv()
        start(y_copy(q, 2))
        y_copy(q, 1).wait_recv()
        start(y_copy(q, 3))

    def near_partner(q):
        start(p_copy(q, 1))
        start(p_copy(q, 2))

    def far_in(q):
        y_copy(q, 2).wait_recv()
        y_copy(q, 3).wait_recv()
        start(p_copy(q, 3))

    def product(q):
        for kind in range(4):
            p_copy(q, kind).wait_recv()

        @pl.loop(0, width // 256)
        def _(n):
            at = pl.ds(pl.multiple_of(n * 256, 256), 256)
            tile = times_transposed(d[q].reshape(ROWS * CHUNK, 2 * hid), w[at, :])
            part[q, :, :, at] = tile.reshape(ROWS, CHUNK, 256)

    half = width // 2

    def z_copy(q, step, minus):
        if step == 0:
            cols = slice(0, half) if minus else slice(half, width)
            src = first.at[q, :, cols]
            dst = (zm if minus else zp).at[q, 0, :, cols]
        else:
            src = (zm if minus else zp).at[q, step - 1]
            dst = (zm if minus else zp).at[q, step]
        side = 0 if minus else 1
        to = (c + NZ - 1) % NZ if minus else (c + 1) % NZ
        return remote(src, dst, z_send.at[q, step, side], z_recv.at[q, step, side], col=to)

    def z_step(q, step):
        if step == 0:
            first[q] = part[q, (c + 4) % NZ].astype(BF16)
        else:
            z_copy(q, step - 1, True).wait_recv()
            before, after = (c + NZ - (4 - step)) % NZ, (c + (4 - step)) % NZ
            if step == 1:
                lo, hi = slice(0, half), slice(half, width)
                zm[q, 0, :, lo] = (zm[q, 0, :, lo].astype(F32) + part[q, before, :, lo]).astype(BF16)
                zm[q, 0, :, hi] = part[q, before, :, hi].astype(BF16)
            else:
                zm[q, step - 1] = (zm[q, step - 1].astype(F32) + part[q, before]).astype(BF16)
        start(z_copy(q, step, True))
        if step > 0:
            z_copy(q, step - 1, False).wait_recv()
            if step == 1:
                zp[q, 0, :, hi] = (zp[q, 0, :, hi].astype(F32) + part[q, after, :, hi]).astype(BF16)
                zp[q, 0, :, lo] = part[q, after, :, lo].astype(BF16)
            else:
                zp[q, step - 1] = (zp[q, step - 1].astype(F32) + part[q, after]).astype(BF16)
        start(z_copy(q, step, False))

    def z_last(q):
        z_copy(q, 3, True).wait_recv()
        z_copy(q, 3, False).wait_recv()
        rows = slice(q * CHUNK, (q + 1) * CHUNK)
        total = part[q, c] + zm[q, 3].astype(F32) + zp[q, 3].astype(F32) + adapter[rows, :]
        out[rows, :] = total.astype(BF16)

    def rank_z(step):
        ref = rank_part.at[c]
        return remote(
            ref, ref, rz_send.at[step - 1], rz_recv.at[step - 1], col=(c + step) % NZ
        )

    def rank_y(step):
        ref = rank_all.at[y, core]
        return remote(ref, ref, ry_send.at[step - 1], ry_recv.at[step - 1], row=row_of(step))

    def rank_p():
        ref = rank_all.at[:, core]
        return remote(ref, ref, rp_send, rp_recv, row=partner)

    def low_s(step):
        to = (r + step) % ROWS
        return remote(
            low_part.at[pl.ds(pl.multiple_of(to * 8, 8), 8), :],
            low_piece.at[step],
            ls_send.at[step - 1],
            ls_recv.at[step - 1],
            row=to,
        )

    def low_g(step):
        ref = low_sum.at[r]
        return remote(ref, ref, lg_send.at[step - 1], lg_recv.at[step - 1], row=(r + step) % ROWS)

    def low_z(step):
        ref = low_all.at[c]
        return remote(ref, ref, lz_send.at[step - 1], lz_recv.at[step - 1], col=(c + step) % NZ)

    def ga_copy(step):
        to = (x + step) % NX
        return remote(
            ga_send.at[to], ga_recv.at[step], ga_ssem.at[step - 1], ga_rsem.at[step - 1], dp=to
        )

    def gb_copy(step):
        to = (x + step) % NX
        return remote(
            gb_send.at[to], gb_recv.at[step], gb_ssem.at[step - 1], gb_rsem.at[step - 1], dp=to
        )

    for load in loads[0:3]:
        load.wait()
    cotangents(0)
    pl.semaphore_wait(barrier, (ROWS - 1) + (NZ - 1) + (NX - 1))
    own(0)
    cotangents(1)
    own(1)
    cotangents(2)
    cotangents(3)
    for q in range(n_chunk):
        start(p_copy(q, 0))

    b[0:64, hid : 2 * hid] = jnp.zeros((64, hid), BF16)
    b[64:128, 0:hid] = jnp.zeros((64, hid), BF16)
    for load in loads[3:8]:
        load.wait()
    rank_part[c] = times_transposed(d[:, r].reshape(own_tok, 2 * hid), b[...]).astype(BF16)
    for step in range(1, NZ):
        start(rank_z(step))
    low_part[...] = times_transposed(act_rows[...], fac[...])
    for step in range(1, ROWS):
        start(low_s(step))

    near(0)
    own(2)
    near_partner(0)

    for step in range(1, NZ):
        rank_z(step).wait_recv()
    rank_all[y, core] = jnp.sum(rank_part[...].astype(F32), axis=0).astype(BF16)
    for step in range(1, NY):
        start(rank_y(step))
    total = low_part[pl.ds(pl.multiple_of(r * 8, 8), 8), :]
    for step in range(1, ROWS):
        low_s(step).wait_recv()
        total = total + low_piece[step]
    low_sum[r] = total
    for step in range(1, ROWS):
        start(low_g(step))

    near(1)
    own(3)
    near_partner(1)

    for step in range(1, ROWS):
        low_g(step).wait_recv()
    low_all[c] = low_sum[...].reshape(own_tok, 128).astype(BF16)
    for step in range(1, NZ):
        start(low_z(step))
    for step in range(1, NY):
        rank_y(step).wait_recv()
    start(rank_p())

    for load in loads[8:]:
        load.wait()
    far_in(0)
    product(0)
    z_step(0, 0)
    near(2)
    near_partner(2)

    rank_p().wait_recv()
    total = factor * lax.dot_general(
        act_cols[...],
        rank_all[...].reshape(group_tok, 128),
        (((0,), (0,)), ((), ())),
        preferred_element_type=F32,
    )
    ga_send[...] = total.reshape(NX, sub // NX, 128)
    for step in range(1, NX):
        start(ga_copy(step))
    adapter[...] = ADAPTER_SCALE * jnp.dot(
        rank_all[c // 2, c % 2], fac[...], preferred_element_type=F32
    )

    z_step(0, 1)
    far_in(1)
    product(1)
    z_step(1, 0)
    z_step(0, 2)
    near(3)
    near_partner(3)
    z_step(1, 1)
    z_step(0, 3)
    far_in(2)
    product(2)
    z_step(2, 0)
    z_step(1, 2)

    for step in range(1, NX):
        ga_copy(step).wait_recv()
    total = ga_send[x]
    for step in range(1, NX):
        total = total + ga_recv[step]
    ga_gate[...] = total[:, 0:64]
    ga_up[...] = total[:, 64:128]
    for step in range(1, NZ):
        low_z(step).wait_recv()

    z_last(0)
    z_step(2, 1)
    z_step(1, 3)
    far_in(3)
    product(3)
    z_step(3, 0)
    z_step(2, 2)

    mine = hid // ROWS
    piece = mine // NX
    window = 384
    base = jnp.minimum((r * mine) // 128 * 128, hid - window)
    shift = r * mine - base
    gate_sum = jnp.zeros((64, window), F32)
    up_sum = jnp.zeros((64, window), F32)
    for q in range(n_chunk):
        low_t = low_all[:, q * CHUNK : (q + 1) * CHUNK, :].reshape(ROWS * CHUNK, 128).T
        gate_sum += jnp.dot(
            low_t[0:64],
            d[q, :, :, pl.ds(pl.multiple_of(base, 128), window)].reshape(ROWS * CHUNK, window),
            preferred_element_type=F32,
        )
        up_sum += jnp.dot(
            low_t[64:128],
            d[q, :, :, pl.ds(pl.multiple_of(hid + base, 128), window)].reshape(
                ROWS * CHUNK, window
            ),
            preferred_element_type=F32,
        )
    gate_sum = factor * gate_sum
    up_sum = factor * up_sum
    lane = lax.broadcasted_iota(jnp.int32, (64, 128), 1)
    for e in range(NX):
        at = shift + e * piece
        gate_at = pltpu.roll(gate_sum, window - at, 1)[:, 0:128]
        up_at = pltpu.roll(up_sum, (window + 64 - at) % window, 1)[:, 0:128]
        gb_send[e] = jnp.where(lane < 64, gate_at, up_at)
    for step in range(1, NX):
        start(gb_copy(step))

    z_step(3, 1)
    z_last(1)
    z_step(2, 3)
    z_step(3, 2)
    for step in range(1, NX):
        gb_copy(step).wait_recv()
    total = gb_send[x]
    for step in range(1, NX):
        total = total + gb_recv[step]
    gb_gate[...] = total[:, 0:piece]
    gb_up[...] = pltpu.roll(total, 64, 1)[:, 0:piece]
    z_step(3, 3)
    z_last(2)
    z_last(3)
    for copy in sent:
        copy.wait_send()


def on_device(
    acts, cot_hidden, gate_pre, up_pre, w_gate, w_up, gate_down_factor, up_down_factor, b_gate, b_up
):
    group_tok, width = acts.shape
    own_tok, hid = cot_hidden.shape
    n_chunk = own_tok // CHUNK
    dma = pltpu.SemaphoreType.DMA
    vmem = pltpu.VMEM
    return pl.pallas_call(
        kernel,
        out_shape=(
            jax.ShapeDtypeStruct((group_tok // NZ, width), BF16),
            jax.ShapeDtypeStruct((width // 32, 64), F32),
            jax.ShapeDtypeStruct((width // 32, 64), F32),
            jax.ShapeDtypeStruct((64, hid // 32), F32),
            jax.ShapeDtypeStruct((64, hid // 32), F32),
        ),
        in_specs=[pl.BlockSpec(memory_space=pl.ANY)] * 10,
        out_specs=tuple([pl.BlockSpec(memory_space=pltpu.VMEM)] * 5),
        scratch_shapes=[
            vmem((3, own_tok, hid), BF16),
            vmem((width, 2 * hid), BF16),
            vmem((128, 2 * hid), BF16),
            vmem((128, width), BF16),
            vmem((own_tok, width), BF16),
            vmem((group_tok, width // NZ), BF16),
            vmem((n_chunk, ROWS, CHUNK, 2 * hid), BF16),
            vmem((n_chunk, ROWS, CHUNK, width), F32),
            vmem((n_chunk, CHUNK, width), BF16),
            vmem((n_chunk, 4, CHUNK, width), BF16),
            vmem((n_chunk, 4, CHUNK, width), BF16),
            vmem((own_tok, width), F32),
            vmem((NZ, own_tok, 128), BF16),
            vmem((NY, 2, own_tok, 128), BF16),
            vmem((own_tok, 128), F32),
            vmem((ROWS, 8, 128), F32),
            vmem((ROWS, 8, 128), F32),
            vmem((NZ, own_tok, 128), BF16),
            vmem((NX, width // 32, 128), F32),
            vmem((NX, width // 32, 128), F32),
            vmem((NX, 64, 128), F32),
            vmem((NX, 64, 128), F32),
            dma((11,)),
            dma((n_chunk, 4)),
            dma((n_chunk, 4)),
            dma((n_chunk, 4)),
            dma((n_chunk, 4)),
            dma((n_chunk, 4, 2)),
            dma((n_chunk, 4, 2)),
            dma((NZ - 1,)),
            dma((NZ - 1,)),
            dma((NY - 1,)),
            dma((NY - 1,)),
            dma,
            dma,
            dma((ROWS - 1,)),
            dma((ROWS - 1,)),
            dma((ROWS - 1,)),
            dma((ROWS - 1,)),
            dma((NZ - 1,)),
            dma((NZ - 1,)),
            dma((NX - 1,)),
            dma((NX - 1,)),
            dma((NX - 1,)),
            dma((NX - 1,)),
        ],
        compiler_params=pltpu.CompilerParams(
            collective_id=0, has_side_effects=True, vmem_limit_bytes=48 * 1024 * 1024
        ),
    )(
        acts,
        cot_hidden,
        gate_pre,
        up_pre,
        w_gate,
        w_up,
        gate_down_factor.T,
        up_down_factor.T,
        b_gate,
        b_up,
    )


def solution(mesh):
    in_specs = (
        P("dp", "row"),
        P(("dp", "row"), "col"),
        P(("dp", "row"), "col"),
        P(("dp", "row"), "col"),
        P("row", "col"),
        P("row", "col"),
        P(),
        P(),
        P(None, "col"),
        P(None, "col"),
    )
    out_specs = (
        P(("dp", "col"), "row"),
        P(("row", "col", "dp"), None),
        P(("row", "col", "dp"), None),
        P(None, ("col", "row", "dp")),
        P(None, ("col", "row", "dp")),
    )
    return jax.shard_map(
        on_device, mesh=mesh, in_specs=in_specs, out_specs=out_specs, check_vma=False
    )
```

```python
import jax
import jax.numpy as jnp
from jax import lax
from jax.experimental import pallas as pl
from jax.experimental.pallas import tpu as pltpu
from jax.sharding import PartitionSpec as P

MESH = pl.DeviceIdType.MESH
F32, BF16 = jnp.float32, jnp.bfloat16
ADAPTER_SCALE = 2.0
NY, NZ, NX = 4, 8, 4
ROWS = 2 * NY
CHUNK = 16


def times_transposed(left, right):
    return lax.dot_general(
        left, right, (((1,), (1,)), ((), ())), preferred_element_type=F32
    )


def kernel(
    acts,
    cot,
    gate_pre,
    up_pre,
    w_gate,
    w_up,
    gate_factor,
    up_factor,
    b_gate,
    b_up,
    out,
    ga_gate,
    ga_up,
    gb_gate,
    gb_up,
    pre,
    w,
    wt,
    b,
    fac,
    act_rows,
    act_cols,
    d,
    part,
    part_send,
    part_recv,
    half_recv,
    adapter,
    rank_part,
    rank_all,
    low_part,
    low_pair,
    low_chip,
    low_recv,
    low_all,
    ga_send,
    ga_recv,
    gb_send,
    gb_recv,
    in_sem,
    y_sem,
    po_sem,
    p_sem,
    z_sem,
    rz_sem,
    ry_sem,
    rp_sem,
    lp_sem,
    ly_sem,
    lz_sem,
    lq_sem,
    ga_sem,
    gb_sem,
):
    own_tok, hid = cot.shape
    group_tok, width = acts.shape
    n_chunk = own_tok // CHUNK
    factor = 2.0 / (group_tok * NX)
    r, c, x = lax.axis_index("row"), lax.axis_index("col"), lax.axis_index("dp")
    y, core = r // 2, r % 2
    sub = width // NZ
    half_tok = own_tok // 2
    near_half = pl.ds(pl.multiple_of(core * half_tok, half_tok), half_tok)
    far_half = pl.ds(pl.multiple_of((1 - core) * half_tok, half_tok), half_tok)

    width_at = pl.multiple_of(r * width, width)
    loads = [
        (cot, pre.at[0]),
        (gate_pre, pre.at[1]),
        (up_pre, pre.at[2]),
        (b_gate, b.at[0:64, 0:hid]),
        (b_up, b.at[64:128, hid : 2 * hid]),
        (acts.at[pl.ds(pl.multiple_of(c * own_tok, own_tok), own_tok), :], act_rows),
        (gate_factor.at[:, pl.ds(width_at, width)], fac.at[0:64]),
        (up_factor.at[:, pl.ds(width_at, width)], fac.at[64:128]),
        (w_gate, w.at[:, 0:hid]),
        (w_up, w.at[:, hid : 2 * hid]),
        (acts.at[:, pl.ds(pl.multiple_of(c * sub, sub), sub)], act_cols),
    ]
    loads = [pltpu.make_async_copy(src, dst, in_sem.at[i]) for i, (src, dst) in enumerate(loads)]
    for load in loads:
        load.start()

    y_peer = [None] + [{"row": ((y + step) % NY) * 2 + core} for step in range(1, NY)]
    z_peer = [None] + [{"col": (c + step) % NZ} for step in range(1, NZ)]
    x_peer = [None] + [{"dp": (x + step) % NX} for step in range(1, NX)]
    partner = {"row": y * 2 + (1 - core)}
    peers = [partner] + y_peer[1:] + z_peer[1:] + x_peer[1:]
    barrier = pltpu.get_barrier_semaphore()
    for peer in peers:
        pl.semaphore_signal(barrier, 1, device_id=peer, device_id_type=MESH)

    sent = []

    def remote(src, dst, sem, where):
        return pltpu.make_async_remote_copy(
            src_ref=src,
            dst_ref=dst,
            send_sem=sem.at[0],
            recv_sem=sem.at[1],
            device_id=where,
            device_id_type=MESH,
        )

    def start(copy):
        copy.start()
        sent.append(copy)

    def cotangents(q):
        rows = slice(q * CHUNK, (q + 1) * CHUNK)
        gate = pre[1, rows, :].astype(F32)
        sig = jax.nn.sigmoid(gate)
        hot = pre[0, rows, :].astype(F32)
        up = pre[2, rows, :].astype(F32)
        d[q, y, core, :, 0:hid] = (hot * up * sig * (1.0 + gate * (1.0 - sig))).astype(BF16)
        d[q, y, core, :, hid : 2 * hid] = (hot * gate * sig).astype(BF16)

    right, left, far = (y + 1) % NY, (y + NY - 1) % NY, (y + 2) % NY

    def y_copy(q, kind):
        ref, step = (
            (d.at[q, y, core], 1),
            (d.at[q, y, core], NY - 1),
            (d.at[q, left, core, :, 0:hid], 1),
            (d.at[q, right, core, :, hid : 2 * hid], NY - 1),
        )[kind]
        return remote(ref, ref, y_sem.at[q, kind], y_peer[step])

    def p_own():
        ref = d.at[:, y, core]
        return remote(ref, ref, po_sem, partner)

    def p_copy(q, kind):
        ref = d.at[q, (left, right, far)[kind], core]
        return remote(ref, ref, p_sem.at[q, kind], partner)

    def own(q):
        start(y_copy(q, 0))
        start(y_copy(q, 1))

    def near(q):
        y_copy(q, 0).wait_recv()
        start(y_copy(q, 2))
        y_copy(q, 1).wait_recv()
        start(y_copy(q, 3))
        if q + 2 < n_chunk:
            own(q + 2)
        start(p_copy(q, 0))
        start(p_copy(q, 1))

    def far_in(q):
        y_copy(q, 2).wait_recv()
        y_copy(q, 3).wait_recv()
        start(p_copy(q, 2))

    def product(q):
        if q == 0:
            p_own().wait_recv()
        for kind in range(NY - 1):
            p_copy(q, kind).wait_recv()
        tile = jnp.dot(
            d[q].reshape(ROWS * CHUNK, 2 * hid), wt[...], preferred_element_type=F32
        ).reshape(ROWS, CHUNK, width)
        part[q] = tile
        part_send[q] = tile.astype(BF16)
        for kind in range(6):
            start(z_copy(q, kind))

    lower, upper = slice(0, width // 2), slice(width // 2, width)

    def z_copy(q, kind):
        sem = z_sem.at[q, kind]
        at = [(c + step) % NZ for step in range(NZ)]
        if kind == 0:
            return remote(part_send.at[q, at[4], :, lower], half_recv.at[q, 0], sem, z_peer[6])
        if kind == 1:
            return remote(part_send.at[q, at[4], :, upper], half_recv.at[q, 1], sem, z_peer[2])
        if kind == 2:
            return remote(part_send.at[q, at[5]], part_recv.at[q, 0], sem, z_peer[7])
        if kind == 3:
            return remote(part_send.at[q, at[3]], part_recv.at[q, 1], sem, z_peer[1])
        if kind == 4:
            return remote(part_send.at[q, at[7]], part_recv.at[q, 2], sem, z_peer[7])
        if kind == 5:
            return remote(part_send.at[q, at[1]], part_recv.at[q, 3], sem, z_peer[1])
        if kind == 6:
            return remote(part_send.at[q, at[6]], part_recv.at[q, 4], sem, z_peer[6])
        return remote(part_send.at[q, at[2]], part_recv.at[q, 5], sem, z_peer[2])

    def z_on(q):
        for side, (same, other, step) in enumerate(((lower, upper, 6), (upper, lower, 2))):
            at = (c + step) % NZ
            z_copy(q, 2 + side).wait_recv()
            z_copy(q, side).wait_recv()
            total = part[q, at, :, same] + part_recv[q, side, :, same].astype(F32)
            total = total + half_recv[q, side].astype(F32)
            part_send[q, at, :, same] = total.astype(BF16)
            total = part[q, at, :, other] + part_recv[q, side, :, other].astype(F32)
            part_send[q, at, :, other] = total.astype(BF16)
            start(z_copy(q, 6 + side))

    def z_last(q):
        rows = slice(q * CHUNK, (q + 1) * CHUNK)
        total = part[q, c] + adapter[rows, :]
        for kind in range(4, 8):
            z_copy(q, kind).wait_recv()
            total = total + part_recv[q, kind - 2].astype(F32)
        out[rows, :] = total.astype(BF16)

    def rank_z(step):
        ref = rank_part.at[c]
        return remote(ref, ref, rz_sem.at[step - 1], z_peer[step])

    def rank_y(step):
        ref = rank_all.at[y, core]
        return remote(ref, ref, ry_sem.at[step - 1], y_peer[step])

    def rank_p():
        ref = rank_all.at[:, core]
        return remote(ref, ref, rp_sem, partner)

    def low_p():
        return remote(low_part.at[far_half], low_pair, lp_sem, partner)

    def low_y(step):
        return remote(low_chip, low_recv.at[step - 1], ly_sem.at[step - 1], y_peer[step])

    def low_z(step):
        ref = low_all.at[c, near_half]
        return remote(ref, ref, lz_sem.at[step - 1], z_peer[step])

    def low_q():
        ref = low_all.at[:, near_half]
        return remote(ref, ref, lq_sem, partner)

    def ga_copy(step):
        return remote(
            ga_send.at[(x + step) % NX], ga_recv.at[step - 1], ga_sem.at[step - 1], x_peer[step]
        )

    def gb_copy(step):
        return remote(
            gb_send.at[(x + step) % NX], gb_recv.at[step - 1], gb_sem.at[step - 1], x_peer[step]
        )

    for load in loads[0:3]:
        load.wait()
    for q in range(n_chunk):
        cotangents(q)
    b[0:64, hid : 2 * hid] = jnp.zeros((64, hid), BF16)
    b[64:128, 0:hid] = jnp.zeros((64, hid), BF16)
    for load in loads[3:8]:
        load.wait()
    rank_part[c] = times_transposed(d[:, y, core].reshape(own_tok, 2 * hid), b[...]).astype(BF16)
    low_part[...] = times_transposed(act_rows[...], fac[...])

    pl.semaphore_wait(barrier, len(peers))
    own(0)
    start(p_own())
    for step in range(1, NZ):
        start(rank_z(step))
    start(low_p())
    own(1)

    for load in loads[8:]:
        load.wait()

    @pl.loop(0, 2 * hid // 256)
    def _(n):
        at = pl.ds(pl.multiple_of(n * 256, 256), 256)
        wt[at, :] = w[:, at].T

    low_p().wait_recv()
    low_own = low_part[near_half, :] + low_pair[...]
    low_chip[...] = low_own.astype(BF16)
    for step in range(1, NY):
        start(low_y(step))
    total = rank_part[c].astype(F32)
    for step in range(1, NZ):
        rank_z(step).wait_recv()
        total = total + rank_part[(c + NZ - step) % NZ].astype(F32)
    rank_all[y, core] = total.astype(BF16)
    for step in range(1, NY):
        start(rank_y(step))

    near(0)
    for step in range(1, NY):
        low_y(step).wait_recv()
        low_own = low_own + low_recv[step - 1].astype(F32)
    low_all[c, near_half] = low_own.astype(BF16)
    for step in range(1, NZ):
        start(low_z(step))
    near(1)
    for step in range(1, NY):
        rank_y(step).wait_recv()
    start(rank_p())
    far_in(0)
    product(0)
    near(2)
    for step in range(1, NZ):
        low_z(step).wait_recv()
    start(low_q())
    far_in(1)
    product(1)

    rank_p().wait_recv()
    total = factor * lax.dot_general(
        act_cols[...],
        rank_all[...].reshape(group_tok, 128),
        (((0,), (0,)), ((), ())),
        preferred_element_type=F32,
    )
    ga_send[...] = total.reshape(NX, sub // NX, 128)
    for step in range(1, NX):
        start(ga_copy(step))
    adapter[...] = ADAPTER_SCALE * jnp.dot(
        rank_all[c // 2, c % 2], fac[...], preferred_element_type=F32
    )

    z_on(0)
    near(3)
    far_in(2)
    product(2)
    z_on(1)
    far_in(3)
    product(3)
    z_on(2)
    low_q().wait_recv()

    mine = hid // ROWS
    piece = mine // NX
    window = 384
    base = jnp.minimum((r * mine) // 128 * 128, hid - window)
    shift = r * mine - base
    gate_sum = jnp.zeros((64, window), F32)
    up_sum = jnp.zeros((64, window), F32)
    for q in range(n_chunk):
        low_t = low_all[:, q * CHUNK : (q + 1) * CHUNK, :].reshape(ROWS * CHUNK, 128).T
        at = pl.ds(pl.multiple_of(base, 128), window)
        gate_sum += jnp.dot(
            low_t[0:64],
            d[q, :, :, :, at].reshape(ROWS * CHUNK, window),
            preferred_element_type=F32,
        )
        at = pl.ds(pl.multiple_of(hid + base, 128), window)
        up_sum += jnp.dot(
            low_t[64:128],
            d[q, :, :, :, at].reshape(ROWS * CHUNK, window),
            preferred_element_type=F32,
        )
    gate_sum = factor * gate_sum
    up_sum = factor * up_sum
    lane = lax.broadcasted_iota(jnp.int32, (64, 128), 1)
    for e in range(NX):
        at = shift + e * piece
        gate_at = pltpu.roll(gate_sum, window - at, 1)[:, 0:128]
        up_at = pltpu.roll(up_sum, (window + 64 - at) % window, 1)[:, 0:128]
        gb_send[e] = jnp.where(lane < 64, gate_at, up_at)
    for step in range(1, NX):
        start(gb_copy(step))

    total = ga_send[x]
    for step in range(1, NX):
        ga_copy(step).wait_recv()
        total = total + ga_recv[step - 1]
    ga_gate[...] = total[:, 0:64]
    ga_up[...] = total[:, 64:128]
    z_last(0)
    z_last(1)
    z_on(3)
    z_last(2)
    total = gb_send[x]
    for step in range(1, NX):
        gb_copy(step).wait_recv()
        total = total + gb_recv[step - 1]
    gb_gate[...] = total[:, 0:piece]
    gb_up[...] = pltpu.roll(total, 64, 1)[:, 0:piece]
    z_last(3)
    for copy in sent:
        copy.wait_send()


def on_device(
    acts, cot_hidden, gate_pre, up_pre, w_gate, w_up, gate_down_factor, up_down_factor, b_gate, b_up
):
    group_tok, width = acts.shape
    own_tok, hid = cot_hidden.shape
    n_chunk = own_tok // CHUNK
    dma = pltpu.SemaphoreType.DMA
    vmem = pltpu.VMEM
    return pl.pallas_call(
        kernel,
        out_shape=(
            jax.ShapeDtypeStruct((group_tok // NZ, width), BF16),
            jax.ShapeDtypeStruct((width // 32, 64), F32),
            jax.ShapeDtypeStruct((width // 32, 64), F32),
            jax.ShapeDtypeStruct((64, hid // 32), F32),
            jax.ShapeDtypeStruct((64, hid // 32), F32),
        ),
        in_specs=[pl.BlockSpec(memory_space=pl.ANY)] * 10,
        out_specs=tuple([pl.BlockSpec(memory_space=pltpu.VMEM)] * 5),
        scratch_shapes=[
            vmem((3, own_tok, hid), BF16),
            vmem((width, 2 * hid), BF16),
            vmem((2 * hid, width), BF16),
            vmem((128, 2 * hid), BF16),
            vmem((128, width), BF16),
            vmem((own_tok, width), BF16),
            vmem((group_tok, width // NZ), BF16),
            vmem((n_chunk, NY, 2, CHUNK, 2 * hid), BF16),
            vmem((n_chunk, ROWS, CHUNK, width), F32),
            vmem((n_chunk, ROWS, CHUNK, width), BF16),
            vmem((n_chunk, 6, CHUNK, width), BF16),
            vmem((n_chunk, 2, CHUNK, width // 2), BF16),
            vmem((own_tok, width), F32),
            vmem((NZ, own_tok, 128), BF16),
            vmem((NY, 2, own_tok, 128), BF16),
            vmem((own_tok, 128), F32),
            vmem((own_tok // 2, 128), F32),
            vmem((own_tok // 2, 128), BF16),
            vmem((NY - 1, own_tok // 2, 128), BF16),
            vmem((NZ, own_tok, 128), BF16),
            vmem((NX, width // 32, 128), F32),
            vmem((NX - 1, width // 32, 128), F32),
            vmem((NX, 64, 128), F32),
            vmem((NX - 1, 64, 128), F32),
            dma((11,)),
            dma((n_chunk, 4, 2)),
            dma((2,)),
            dma((n_chunk, NY - 1, 2)),
            dma((n_chunk, 8, 2)),
            dma((NZ - 1, 2)),
            dma((NY - 1, 2)),
            dma((2,)),
            dma((2,)),
            dma((NY - 1, 2)),
            dma((NZ - 1, 2)),
            dma((2,)),
            dma((NX - 1, 2)),
            dma((NX - 1, 2)),
        ],
        compiler_params=pltpu.CompilerParams(
            collective_id=0, has_side_effects=True, vmem_limit_bytes=60 * 1024 * 1024
        ),
    )(
        acts,
        cot_hidden,
        gate_pre,
        up_pre,
        w_gate,
        w_up,
        gate_down_factor.T,
        up_down_factor.T,
        b_gate,
        b_up,
    )


def solution(mesh):
    in_specs = (
        P("dp", "row"),
        P(("dp", "row"), "col"),
        P(("dp", "row"), "col"),
        P(("dp", "row"), "col"),
        P("row", "col"),
        P("row", "col"),
        P(),
        P(),
        P(None, "col"),
        P(None, "col"),
    )
    out_specs = (
        P(("dp", "col"), "row"),
        P(("row", "col", "dp"), None),
        P(("row", "col", "dp"), None),
        P(None, ("col", "row", "dp")),
        P(None, ("col", "row", "dp")),
    )
    return jax.shard_map(
        on_device, mesh=mesh, in_specs=in_specs, out_specs=out_specs, check_vma=False
    )
```

```python
import jax
import jax.numpy as jnp
from jax import lax
from jax.experimental import pallas as pl
from jax.experimental.pallas import tpu as pltpu
from jax.sharding import PartitionSpec as P

MESH = pl.DeviceIdType.MESH
F32, BF16 = jnp.float32, jnp.bfloat16
ADAPTER_SCALE = 2.0
NY, NZ, NX = 4, 8, 4
ROWS = 2 * NY
CHUNK = 16


def times_transposed(left, right):
    return lax.dot_general(
        left, right, (((1,), (1,)), ((), ())), preferred_element_type=F32
    )


def kernel(
    acts,
    cot,
    gate_pre,
    up_pre,
    w_gate,
    w_up,
    gate_factor,
    up_factor,
    b_gate,
    b_up,
    out,
    small,
    pre,
    w,
    wt,
    b,
    fac,
    act_rows,
    act_cols,
    d,
    part,
    part_send,
    part_recv,
    half_recv,
    adapter,
    rank_part,
    rank_all,
    low_part,
    low_pair,
    low_chip,
    low_recv,
    low_all,
    ga_send,
    ga_recv,
    gb_send,
    gb_recv,
    in_sem,
    y_sem,
    po_sem,
    p_sem,
    z_sem,
    rz_sem,
    ry_sem,
    rp_sem,
    lp_sem,
    ly_sem,
    lz_sem,
    lq_sem,
    ga_sem,
    gb_sem,
):
    own_tok, hid = cot.shape
    group_tok, width = acts.shape
    n_chunk = own_tok // CHUNK
    factor = 2.0 / (group_tok * NX)
    r, c, x = lax.axis_index("row"), lax.axis_index("col"), lax.axis_index("dp")
    y, core = r // 2, r % 2
    sub = width // NZ
    half_tok = own_tok // 2
    near_half = pl.ds(pl.multiple_of(core * half_tok, half_tok), half_tok)
    far_half = pl.ds(pl.multiple_of((1 - core) * half_tok, half_tok), half_tok)

    width_at = pl.multiple_of(r * width, width)
    loads = [
        (cot, pre.at[0]),
        (gate_pre, pre.at[1]),
        (up_pre, pre.at[2]),
        (b_gate, b.at[0:64, 0:hid]),
        (b_up, b.at[64:128, hid : 2 * hid]),
        (acts.at[pl.ds(pl.multiple_of(c * own_tok, own_tok), own_tok), :], act_rows),
        (gate_factor.at[:, pl.ds(width_at, width)], fac.at[0:64]),
        (up_factor.at[:, pl.ds(width_at, width)], fac.at[64:128]),
        (w_gate, w.at[:, 0:hid]),
        (w_up, w.at[:, hid : 2 * hid]),
        (acts.at[:, pl.ds(pl.multiple_of(c * sub, sub), sub)], act_cols),
    ]
    loads = [pltpu.make_async_copy(src, dst, in_sem.at[i]) for i, (src, dst) in enumerate(loads)]
    for load in loads[0:8]:
        load.start()

    y_peer = [None] + [{"row": ((y + step) % NY) * 2 + core} for step in range(1, NY)]
    z_peer = [None] + [{"col": (c + step) % NZ} for step in range(1, NZ)]
    x_peer = [None] + [{"dp": (x + step) % NX} for step in range(1, NX)]
    partner = {"row": y * 2 + (1 - core)}
    peers = [partner] + y_peer[1:] + z_peer[1:] + x_peer[1:]
    barrier = pltpu.get_barrier_semaphore()
    for peer in peers:
        pl.semaphore_signal(barrier, 1, device_id=peer, device_id_type=MESH)

    sent = []

    def remote(src, dst, sem, where):
        return pltpu.make_async_remote_copy(
            src_ref=src,
            dst_ref=dst,
            send_sem=sem.at[0],
            recv_sem=sem.at[1],
            device_id=where,
            device_id_type=MESH,
        )

    def start(copy):
        copy.start()
        sent.append(copy)

    def cotangents(q):
        rows = slice(q * CHUNK, (q + 1) * CHUNK)
        gate = pre[1, rows, :].astype(F32)
        sig = jax.nn.sigmoid(gate)
        hot = pre[0, rows, :].astype(F32)
        up = pre[2, rows, :].astype(F32)
        d[q, y, core, :, 0:hid] = (hot * up * sig * (1.0 + gate * (1.0 - sig))).astype(BF16)
        d[q, y, core, :, hid : 2 * hid] = (hot * gate * sig).astype(BF16)

    right, left, far = (y + 1) % NY, (y + NY - 1) % NY, (y + 2) % NY

    def y_copy(q, kind):
        gate, up = slice(0, hid), slice(hid, 2 * hid)
        ref, step = (
            (d.at[q, y, core, :, gate], 1),
            (d.at[q, y, core, :, up], NY - 1),
            (d.at[q, y, core, :, up], 1),
            (d.at[q, y, core, :, gate], NY - 1),
            (d.at[q, left, core, :, gate], 1),
            (d.at[q, right, core, :, up], NY - 1),
        )[kind]
        return remote(ref, ref, y_sem.at[q, kind], y_peer[step])

    def p_own():
        ref = d.at[:, y, core]
        return remote(ref, ref, po_sem, partner)

    def p_copy(q, kind):
        ref = d.at[q, (left, right, far)[kind], core]
        return remote(ref, ref, p_sem.at[q, kind], partner)

    def own(q):
        for kind in range(4):
            start(y_copy(q, kind))

    def near(q):
        y_copy(q, 0).wait_recv()
        start(y_copy(q, 4))
        y_copy(q, 1).wait_recv()
        start(y_copy(q, 5))
        if q + 2 < n_chunk:
            own(q + 2)
        y_copy(q, 2).wait_recv()
        y_copy(q, 3).wait_recv()
        start(p_copy(q, 0))
        start(p_copy(q, 1))

    def far_in(q):
        y_copy(q, 4).wait_recv()
        y_copy(q, 5).wait_recv()
        start(p_copy(q, 2))

    def product(q):
        if q == 0:
            p_own().wait_recv()
        for kind in range(NY - 1):
            p_copy(q, kind).wait_recv()
        tile = jnp.dot(
            d[q].reshape(ROWS * CHUNK, 2 * hid), wt[...], preferred_element_type=F32
        ).reshape(ROWS, CHUNK, width)
        part[q] = tile
        part_send[q] = tile.astype(BF16)
        for kind in range(6):
            start(z_copy(q, kind))

    lower, upper = slice(0, width // 2), slice(width // 2, width)

    def z_copy(q, kind):
        sem = z_sem.at[q, kind]
        at = [(c + step) % NZ for step in range(NZ)]
        if kind == 0:
            return remote(part_send.at[q, at[4], :, lower], half_recv.at[q, 0], sem, z_peer[6])
        if kind == 1:
            return remote(part_send.at[q, at[4], :, upper], half_recv.at[q, 1], sem, z_peer[2])
        if kind == 2:
            return remote(part_send.at[q, at[5]], part_recv.at[q, 0], sem, z_peer[7])
        if kind == 3:
            return remote(part_send.at[q, at[3]], part_recv.at[q, 1], sem, z_peer[1])
        if kind == 4:
            return remote(part_send.at[q, at[7]], part_recv.at[q, 2], sem, z_peer[7])
        if kind == 5:
            return remote(part_send.at[q, at[1]], part_recv.at[q, 3], sem, z_peer[1])
        if kind == 6:
            return remote(part_send.at[q, at[6]], part_recv.at[q, 4], sem, z_peer[6])
        return remote(part_send.at[q, at[2]], part_recv.at[q, 5], sem, z_peer[2])

    def z_on(q):
        for side, (same, other, step) in enumerate(((lower, upper, 6), (upper, lower, 2))):
            at = (c + step) % NZ
            z_copy(q, 2 + side).wait_recv()
            z_copy(q, side).wait_recv()
            total = part[q, at, :, same] + part_recv[q, side, :, same].astype(F32)
            total = total + half_recv[q, side].astype(F32)
            part_send[q, at, :, same] = total.astype(BF16)
            total = part[q, at, :, other] + part_recv[q, side, :, other].astype(F32)
            part_send[q, at, :, other] = total.astype(BF16)
            start(z_copy(q, 6 + side))

    def z_last(q):
        rows = slice(q * CHUNK, (q + 1) * CHUNK)
        total = part[q, c] + adapter[rows, :]
        for kind in range(4, 8):
            z_copy(q, kind).wait_recv()
            total = total + part_recv[q, kind - 2].astype(F32)
        out[rows, :] = total.astype(BF16)

    def rank_z(step):
        ref = rank_part.at[c]
        return remote(ref, ref, rz_sem.at[step - 1], z_peer[step])

    def rank_y(step):
        ref = rank_all.at[y, core]
        return remote(ref, ref, ry_sem.at[step - 1], y_peer[step])

    def rank_p():
        ref = rank_all.at[:, core]
        return remote(ref, ref, rp_sem, partner)

    def low_p():
        return remote(low_part.at[far_half], low_pair, lp_sem, partner)

    def low_y(step):
        return remote(low_chip, low_recv.at[step - 1], ly_sem.at[step - 1], y_peer[step])

    def low_z(step):
        ref = low_all.at[c, near_half]
        return remote(ref, ref, lz_sem.at[step - 1], z_peer[step])

    def low_q():
        ref = low_all.at[:, near_half]
        return remote(ref, ref, lq_sem, partner)

    def ga_copy(step):
        return remote(
            ga_send.at[(x + step) % NX], ga_recv.at[step - 1], ga_sem.at[step - 1], x_peer[step]
        )

    def gb_copy(step):
        return remote(
            gb_send.at[(x + step) % NX], gb_recv.at[step - 1], gb_sem.at[step - 1], x_peer[step]
        )

    for load in loads[0:3]:
        load.wait()
    for load in loads[8:]:
        load.start()
    cotangents(0)
    pl.semaphore_wait(barrier, len(peers))
    own(0)
    cotangents(1)
    own(1)
    cotangents(2)
    cotangents(3)
    start(p_own())
    b[0:64, hid : 2 * hid] = jnp.zeros((64, hid), BF16)
    b[64:128, 0:hid] = jnp.zeros((64, hid), BF16)
    for load in loads[3:8]:
        load.wait()
    low_part[...] = times_transposed(act_rows[...], fac[...])
    start(low_p())
    rank_part[c] = times_transposed(d[:, y, core].reshape(own_tok, 2 * hid), b[...]).astype(BF16)
    for step in range(1, NZ):
        start(rank_z(step))

    low_p().wait_recv()
    low_own = low_part[near_half, :] + low_pair[...]
    low_chip[...] = low_own.astype(BF16)
    for step in range(1, NY):
        start(low_y(step))
    near(0)

    for load in loads[8:]:
        load.wait()

    @pl.loop(0, 2 * hid // 256)
    def _(n):
        at = pl.ds(pl.multiple_of(n * 256, 256), 256)
        wt[at, :] = w[:, at].T

    near(1)
    for step in range(1, NY):
        low_y(step).wait_recv()
        low_own = low_own + low_recv[step - 1].astype(F32)
    low_all[c, near_half] = low_own.astype(BF16)
    for step in range(1, NZ):
        start(low_z(step))
    far_in(0)
    product(0)
    total = rank_part[c].astype(F32)
    for step in range(1, NZ):
        rank_z(step).wait_recv()
        total = total + rank_part[(c + NZ - step) % NZ].astype(F32)
    rank_all[y, core] = total.astype(BF16)
    for step in range(1, NY):
        start(rank_y(step))
    near(2)
    far_in(1)
    product(1)
    near(3)
    for step in range(1, NZ):
        low_z(step).wait_recv()
    start(low_q())
    far_in(2)
    z_on(0)
    far_in(3)
    product(2)
    product(3)
    for step in range(1, NY):
        rank_y(step).wait_recv()
    start(rank_p())
    z_on(1)
    low_q().wait_recv()

    mine = hid // ROWS
    piece = mine // NX
    window = 384
    base = jnp.minimum((r * mine) // 128 * 128, hid - window)
    shift = r * mine - base
    gate_sum = jnp.zeros((64, window), F32)
    up_sum = jnp.zeros((64, window), F32)
    for q in range(n_chunk):
        low_t = low_all[:, q * CHUNK : (q + 1) * CHUNK, :].reshape(ROWS * CHUNK, 128).T
        at = pl.ds(pl.multiple_of(base, 128), window)
        gate_sum += jnp.dot(
            low_t[0:64],
            d[q, :, :, :, at].reshape(ROWS * CHUNK, window),
            preferred_element_type=F32,
        )
        at = pl.ds(pl.multiple_of(hid + base, 128), window)
        up_sum += jnp.dot(
            low_t[64:128],
            d[q, :, :, :, at].reshape(ROWS * CHUNK, window),
            preferred_element_type=F32,
        )
    gate_sum = factor * gate_sum
    up_sum = factor * up_sum
    lane = lax.broadcasted_iota(jnp.int32, (64, 128), 1)
    for e in range(NX):
        at = shift + e * piece
        gate_at = pltpu.roll(gate_sum, window - at, 1)[:, 0:128]
        up_at = pltpu.roll(up_sum, (window + 64 - at) % window, 1)[:, 0:128]
        gb_send[e] = jnp.where(lane < 64, gate_at, up_at)
    for step in range(1, NX):
        start(gb_copy(step))

    rank_p().wait_recv()
    total = factor * lax.dot_general(
        act_cols[...],
        rank_all[...].reshape(group_tok, 128),
        (((0,), (0,)), ((), ())),
        preferred_element_type=F32,
    )
    ga_send[...] = total.reshape(NX, sub // NX, 128)
    for step in range(1, NX):
        start(ga_copy(step))
    adapter[...] = ADAPTER_SCALE * jnp.dot(
        rank_all[c // 2, c % 2], fac[...], preferred_element_type=F32
    )

    z_on(2)
    z_last(0)
    z_last(1)
    z_on(3)
    total = gb_send[x]
    for step in range(1, NX):
        gb_copy(step).wait_recv()
        total = total + gb_recv[step - 1]
    small[sub // NX :, :] = total
    total = ga_send[x]
    for step in range(1, NX):
        ga_copy(step).wait_recv()
        total = total + ga_recv[step - 1]
    small[0 : sub // NX, :] = total
    z_last(2)
    z_last(3)
    for copy in sent:
        copy.wait_send()


def place(out_in, small, out, ga_gate, ga_up, gb_gate, gb_up):
    rows, piece = ga_gate.shape[0], gb_gate.shape[1]
    out[...] = out_in[...]
    ga_gate[...] = small[0:rows, 0:64]
    ga_up[...] = small[0:rows, 64:128]
    gb_gate[...] = small[rows:, 0:piece]
    gb_up[...] = pltpu.roll(small[rows:, :], 64, 1)[:, 0:piece]


def on_device(
    acts, cot_hidden, gate_pre, up_pre, w_gate, w_up, gate_down_factor, up_down_factor, b_gate, b_up
):
    group_tok, width = acts.shape
    own_tok, hid = cot_hidden.shape
    n_chunk = own_tok // CHUNK
    dma = pltpu.SemaphoreType.DMA
    vmem = pltpu.VMEM
    shapes = (
        jax.ShapeDtypeStruct((group_tok // NZ, width), BF16),
        jax.ShapeDtypeStruct((width // 32, 64), F32),
        jax.ShapeDtypeStruct((width // 32, 64), F32),
        jax.ShapeDtypeStruct((64, hid // 32), F32),
        jax.ShapeDtypeStruct((64, hid // 32), F32),
    )
    results = pl.pallas_call(
        kernel,
        out_shape=(shapes[0], jax.ShapeDtypeStruct((width // 32 + 64, 128), F32)),
        in_specs=[pl.BlockSpec(memory_space=pl.ANY)] * 10,
        out_specs=(pl.BlockSpec(memory_space=pltpu.VMEM),) * 2,
        scratch_shapes=[
            vmem((3, own_tok, hid), BF16),
            vmem((width, 2 * hid), BF16),
            vmem((2 * hid, width), BF16),
            vmem((128, 2 * hid), BF16),
            vmem((128, width), BF16),
            vmem((own_tok, width), BF16),
            vmem((group_tok, width // NZ), BF16),
            vmem((n_chunk, NY, 2, CHUNK, 2 * hid), BF16),
            vmem((n_chunk, ROWS, CHUNK, width), F32),
            vmem((n_chunk, ROWS, CHUNK, width), BF16),
            vmem((n_chunk, 6, CHUNK, width), BF16),
            vmem((n_chunk, 2, CHUNK, width // 2), BF16),
            vmem((own_tok, width), F32),
            vmem((NZ, own_tok, 128), BF16),
            vmem((NY, 2, own_tok, 128), BF16),
            vmem((own_tok, 128), F32),
            vmem((own_tok // 2, 128), F32),
            vmem((own_tok // 2, 128), BF16),
            vmem((NY - 1, own_tok // 2, 128), BF16),
            vmem((NZ, own_tok, 128), BF16),
            vmem((NX, width // 32, 128), F32),
            vmem((NX - 1, width // 32, 128), F32),
            vmem((NX, 64, 128), F32),
            vmem((NX - 1, 64, 128), F32),
            dma((11,)),
            dma((n_chunk, 6, 2)),
            dma((2,)),
            dma((n_chunk, NY - 1, 2)),
            dma((n_chunk, 8, 2)),
            dma((NZ - 1, 2)),
            dma((NY - 1, 2)),
            dma((2,)),
            dma((2,)),
            dma((NY - 1, 2)),
            dma((NZ - 1, 2)),
            dma((2,)),
            dma((NX - 1, 2)),
            dma((NX - 1, 2)),
        ],
        compiler_params=pltpu.CompilerParams(
            collective_id=0, has_side_effects=True, vmem_limit_bytes=60 * 1024 * 1024
        ),
    )(
        acts,
        cot_hidden,
        gate_pre,
        up_pre,
        w_gate,
        w_up,
        gate_down_factor.T,
        up_down_factor.T,
        b_gate,
        b_up,
    )
    return pl.pallas_call(
        place,
        out_shape=shapes,
        in_specs=[pl.BlockSpec(memory_space=pltpu.VMEM)] * 2,
        out_specs=(pl.BlockSpec(memory_space=pltpu.VMEM),) * 5,
    )(*results)


def solution(mesh):
    in_specs = (
        P("dp", "row"),
        P(("dp", "row"), "col"),
        P(("dp", "row"), "col"),
        P(("dp", "row"), "col"),
        P("row", "col"),
        P("row", "col"),
        P(),
        P(),
        P(None, "col"),
        P(None, "col"),
    )
    out_specs = (
        P(("dp", "col"), "row"),
        P(("row", "col", "dp"), None),
        P(("row", "col", "dp"), None),
        P(None, ("col", "row", "dp")),
        P(None, ("col", "row", "dp")),
    )
    return jax.shard_map(
        on_device, mesh=mesh, in_specs=in_specs, out_specs=out_specs, check_vma=False
    )
```

```python
import jax
import jax.numpy as jnp
from jax import lax
from jax.experimental import pallas as pl
from jax.experimental.pallas import tpu as pltpu
from jax.sharding import PartitionSpec as P

MESH = pl.DeviceIdType.MESH
F32, BF16 = jnp.float32, jnp.bfloat16
ADAPTER_SCALE = 2.0
NY, NZ, NX = 4, 8, 4
ROWS = 2 * NY
CHUNK = 16


def times_transposed(left, right):
    return lax.dot_general(
        left, right, (((1,), (1,)), ((), ())), preferred_element_type=F32
    )


def kernel(
    acts,
    cot,
    gate_pre,
    up_pre,
    w_gate,
    w_up,
    gate_factor,
    up_factor,
    b_gate,
    b_up,
    out,
    small,
    pre,
    w,
    wt,
    b,
    fac,
    act_rows,
    act_cols,
    d,
    part,
    part_send,
    part_recv,
    half_recv,
    adapter,
    rank_part,
    rank_all,
    low_part,
    low_pair,
    low_chip,
    low_recv,
    low_all,
    ga_send,
    ga_recv,
    gb_send,
    gb_recv,
    in_sem,
    y_sem,
    po_sem,
    p_sem,
    z_sem,
    rz_sem,
    ry_sem,
    rp_sem,
    lp_sem,
    ly_sem,
    lz_sem,
    lq_sem,
    ga_sem,
    gb_sem,
):
    own_tok, hid = cot.shape
    group_tok, width = acts.shape
    n_chunk = own_tok // CHUNK
    factor = 2.0 / (group_tok * NX)
    r, c, x = lax.axis_index("row"), lax.axis_index("col"), lax.axis_index("dp")
    y, core = r // 2, r % 2
    sub = width // NZ
    half_tok = own_tok // 2
    near_half = pl.ds(pl.multiple_of(core * half_tok, half_tok), half_tok)
    far_half = pl.ds(pl.multiple_of((1 - core) * half_tok, half_tok), half_tok)

    width_at = pl.multiple_of(r * width, width)
    loads = [
        (cot, pre.at[0]),
        (gate_pre, pre.at[1]),
        (up_pre, pre.at[2]),
        (b_gate, b.at[0:64, 0:hid]),
        (b_up, b.at[64:128, hid : 2 * hid]),
        (acts.at[pl.ds(pl.multiple_of(c * own_tok, own_tok), own_tok), :], act_rows),
        (gate_factor.at[:, pl.ds(width_at, width)], fac.at[0:64]),
        (up_factor.at[:, pl.ds(width_at, width)], fac.at[64:128]),
        (w_gate, w.at[:, 0:hid]),
        (w_up, w.at[:, hid : 2 * hid]),
        (acts.at[:, pl.ds(pl.multiple_of(c * sub, sub), sub)], act_cols),
    ]
    loads = [pltpu.make_async_copy(src, dst, in_sem.at[i]) for i, (src, dst) in enumerate(loads)]
    for load in loads[0:8]:
        load.start()

    y_peer = [None] + [{"row": ((y + step) % NY) * 2 + core} for step in range(1, NY)]
    z_peer = [None] + [{"col": (c + step) % NZ} for step in range(1, NZ)]
    x_peer = [None] + [{"dp": (x + step) % NX} for step in range(1, NX)]
    partner = {"row": y * 2 + (1 - core)}
    peers = [partner] + y_peer[1:] + z_peer[1:] + x_peer[1:]
    barrier = pltpu.get_barrier_semaphore()
    for peer in peers:
        pl.semaphore_signal(barrier, 1, device_id=peer, device_id_type=MESH)

    sent = []

    def remote(src, dst, sem, where):
        return pltpu.make_async_remote_copy(
            src_ref=src,
            dst_ref=dst,
            send_sem=sem.at[0],
            recv_sem=sem.at[1],
            device_id=where,
            device_id_type=MESH,
        )

    def start(copy):
        copy.start()
        sent.append(copy)

    def cotangents(q):
        rows = slice(q * CHUNK, (q + 1) * CHUNK)
        gate = pre[1, rows, :].astype(F32)
        sig = jax.nn.sigmoid(gate)
        hot = pre[0, rows, :].astype(F32)
        up = pre[2, rows, :].astype(F32)
        d[q, y, core, :, 0:hid] = (hot * up * sig * (1.0 + gate * (1.0 - sig))).astype(BF16)
        d[q, y, core, :, hid : 2 * hid] = (hot * gate * sig).astype(BF16)

    right, left, far = (y + 1) % NY, (y + NY - 1) % NY, (y + 2) % NY

    def y_copy(q, kind):
        gate, up = slice(0, hid), slice(hid, 2 * hid)
        ref, step = (
            (d.at[q, y, core, :, gate], 1),
            (d.at[q, y, core, :, up], NY - 1),
            (d.at[q, y, core, :, up], 1),
            (d.at[q, y, core, :, gate], NY - 1),
            (d.at[q, left, core, :, gate], 1),
            (d.at[q, right, core, :, up], NY - 1),
        )[kind]
        return remote(ref, ref, y_sem.at[q, kind], y_peer[step])

    def p_own():
        ref = d.at[:, y, core]
        return remote(ref, ref, po_sem, partner)

    def p_copy(q, kind):
        ref = d.at[q, (left, right, far)[kind], core]
        return remote(ref, ref, p_sem.at[q, kind], partner)

    def own(q):
        for kind in range(4):
            start(y_copy(q, kind))

    def near(q):
        y_copy(q, 0).wait_recv()
        start(y_copy(q, 4))
        y_copy(q, 1).wait_recv()
        start(y_copy(q, 5))
        if q + 2 < n_chunk:
            own(q + 2)
        y_copy(q, 2).wait_recv()
        y_copy(q, 3).wait_recv()
        start(p_copy(q, 0))
        start(p_copy(q, 1))

    def far_in(q):
        y_copy(q, 4).wait_recv()
        y_copy(q, 5).wait_recv()
        start(p_copy(q, 2))

    def product(q):
        if q == 0:
            p_own().wait_recv()
        for kind in range(NY - 1):
            p_copy(q, kind).wait_recv()
        tile = jnp.dot(
            d[q].reshape(ROWS * CHUNK, 2 * hid), wt[...], preferred_element_type=F32
        ).reshape(ROWS, CHUNK, width)
        part[q] = tile
        part_send[q] = tile.astype(BF16)
        for kind in range(6):
            start(z_copy(q, kind))

    lower, upper = slice(0, width // 2), slice(width // 2, width)

    def z_copy(q, kind):
        sem = z_sem.at[q, kind]
        at = [(c + step) % NZ for step in range(NZ)]
        if kind == 0:
            return remote(part_send.at[q, at[4], :, lower], half_recv.at[q, 0], sem, z_peer[6])
        if kind == 1:
            return remote(part_send.at[q, at[4], :, upper], half_recv.at[q, 1], sem, z_peer[2])
        if kind == 2:
            return remote(part_send.at[q, at[5]], part_recv.at[q, 0], sem, z_peer[7])
        if kind == 3:
            return remote(part_send.at[q, at[3]], part_recv.at[q, 1], sem, z_peer[1])
        if kind == 4:
            return remote(part_send.at[q, at[7]], part_recv.at[q, 2], sem, z_peer[7])
        if kind == 5:
            return remote(part_send.at[q, at[1]], part_recv.at[q, 3], sem, z_peer[1])
        if kind == 6:
            return remote(part_send.at[q, at[6]], part_recv.at[q, 4], sem, z_peer[6])
        return remote(part_send.at[q, at[2]], part_recv.at[q, 5], sem, z_peer[2])

    def z_on(q):
        for side, (same, other, step) in enumerate(((lower, upper, 6), (upper, lower, 2))):
            at = (c + step) % NZ
            z_copy(q, 2 + side).wait_recv()
            z_copy(q, side).wait_recv()
            total = part[q, at, :, same] + part_recv[q, side, :, same].astype(F32)
            total = total + half_recv[q, side].astype(F32)
            part_send[q, at, :, same] = total.astype(BF16)
            total = part[q, at, :, other] + part_recv[q, side, :, other].astype(F32)
            part_send[q, at, :, other] = total.astype(BF16)
            start(z_copy(q, 6 + side))

    def z_last(q):
        rows = slice(q * CHUNK, (q + 1) * CHUNK)
        total = part[q, c] + adapter[rows, :]
        for kind in range(4, 8):
            z_copy(q, kind).wait_recv()
            total = total + part_recv[q, kind - 2].astype(F32)
        out[rows, :] = total.astype(BF16)

    def rank_z(step):
        ref = rank_part.at[c]
        return remote(ref, ref, rz_sem.at[step - 1], z_peer[step])

    def rank_y(step):
        ref = rank_all.at[y, core]
        return remote(ref, ref, ry_sem.at[step - 1], y_peer[step])

    def rank_p():
        ref = rank_all.at[:, core]
        return remote(ref, ref, rp_sem, partner)

    def low_p():
        return remote(low_part.at[far_half], low_pair, lp_sem, partner)

    def low_y(step):
        return remote(low_chip, low_recv.at[step - 1], ly_sem.at[step - 1], y_peer[step])

    def low_z(step):
        ref = low_all.at[c, near_half]
        return remote(ref, ref, lz_sem.at[step - 1], z_peer[step])

    def low_q():
        ref = low_all.at[:, near_half]
        return remote(ref, ref, lq_sem, partner)

    def ga_copy(step):
        return remote(
            ga_send.at[(x + step) % NX], ga_recv.at[step - 1], ga_sem.at[step - 1], x_peer[step]
        )

    def gb_copy(step):
        return remote(
            gb_send.at[(x + step) % NX], gb_recv.at[step - 1], gb_sem.at[step - 1], x_peer[step]
        )

    for load in loads[0:3]:
        load.wait()
    for load in loads[8:]:
        load.start()
    cotangents(0)
    pl.semaphore_wait(barrier, len(peers))
    own(0)
    cotangents(1)
    own(1)
    cotangents(2)
    cotangents(3)
    start(p_own())
    b[0:64, hid : 2 * hid] = jnp.zeros((64, hid), BF16)
    b[64:128, 0:hid] = jnp.zeros((64, hid), BF16)
    for load in loads[3:8]:
        load.wait()
    low_part[...] = times_transposed(act_rows[...], fac[...])
    start(low_p())
    rank_part[c] = times_transposed(d[:, y, core].reshape(own_tok, 2 * hid), b[...]).astype(BF16)
    for step in range(1, NZ):
        start(rank_z(step))

    low_p().wait_recv()
    low_own = low_part[near_half, :] + low_pair[...]
    low_chip[...] = low_own.astype(BF16)
    for step in range(1, NY):
        start(low_y(step))
    near(0)

    for load in loads[8:]:
        load.wait()

    @pl.loop(0, 2 * hid // 256)
    def _(n):
        at = pl.ds(pl.multiple_of(n * 256, 256), 256)
        wt[at, :] = w[:, at].T

    near(1)
    for step in range(1, NY):
        low_y(step).wait_recv()
        low_own = low_own + low_recv[step - 1].astype(F32)
    low_all[c, near_half] = low_own.astype(BF16)
    for step in range(1, NZ):
        start(low_z(step))
    far_in(0)
    product(0)
    total = rank_part[c].astype(F32)
    for step in range(1, NZ):
        rank_z(step).wait_recv()
        total = total + rank_part[(c + NZ - step) % NZ].astype(F32)
    rank_all[y, core] = total.astype(BF16)
    for step in range(1, NY):
        start(rank_y(step))
    near(2)
    far_in(1)
    product(1)
    z_on(0)
    near(3)
    far_in(2)
    product(2)
    for step in range(1, NZ):
        low_z(step).wait_recv()
    start(low_q())
    for step in range(1, NY):
        rank_y(step).wait_recv()
    start(rank_p())
    z_on(1)
    far_in(3)
    product(3)
    low_q().wait_recv()

    mine = hid // ROWS
    piece = mine // NX
    window = 384
    base = jnp.minimum((r * mine) // 128 * 128, hid - window)
    shift = r * mine - base
    gate_sum = jnp.zeros((64, window), F32)
    up_sum = jnp.zeros((64, window), F32)
    for q in range(n_chunk):
        low_t = low_all[:, q * CHUNK : (q + 1) * CHUNK, :].reshape(ROWS * CHUNK, 128).T
        at = pl.ds(pl.multiple_of(base, 128), window)
        gate_sum += jnp.dot(
            low_t[0:64],
            d[q, :, :, :, at].reshape(ROWS * CHUNK, window),
            preferred_element_type=F32,
        )
        at = pl.ds(pl.multiple_of(hid + base, 128), window)
        up_sum += jnp.dot(
            low_t[64:128],
            d[q, :, :, :, at].reshape(ROWS * CHUNK, window),
            preferred_element_type=F32,
        )
    gate_sum = factor * gate_sum
    up_sum = factor * up_sum
    lane = lax.broadcasted_iota(jnp.int32, (64, 128), 1)
    for e in range(NX):
        at = shift + e * piece
        gate_at = pltpu.roll(gate_sum, window - at, 1)[:, 0:128]
        up_at = pltpu.roll(up_sum, (window + 64 - at) % window, 1)[:, 0:128]
        gb_send[e] = jnp.where(lane < 64, gate_at, up_at)
    for step in range(1, NX):
        start(gb_copy(step))

    rank_p().wait_recv()
    total = factor * lax.dot_general(
        act_cols[...],
        rank_all[...].reshape(group_tok, 128),
        (((0,), (0,)), ((), ())),
        preferred_element_type=F32,
    )
    ga_send[...] = total.reshape(NX, sub // NX, 128)
    for step in range(1, NX):
        start(ga_copy(step))
    adapter[...] = ADAPTER_SCALE * jnp.dot(
        rank_all[c // 2, c % 2], fac[...], preferred_element_type=F32
    )

    z_on(2)
    z_last(0)
    z_last(1)
    z_on(3)
    total = gb_send[x]
    for step in range(1, NX):
        gb_copy(step).wait_recv()
        total = total + gb_recv[step - 1]
    small[sub // NX :, :] = total
    total = ga_send[x]
    for step in range(1, NX):
        ga_copy(step).wait_recv()
        total = total + ga_recv[step - 1]
    small[0 : sub // NX, :] = total
    z_last(2)
    z_last(3)
    for copy in sent:
        copy.wait_send()


def place(out_in, small, out, ga_gate, ga_up, gb_gate, gb_up):
    rows, piece = ga_gate.shape[0], gb_gate.shape[1]
    out[...] = out_in[...]
    ga_gate[...] = small[0:rows, 0:64]
    ga_up[...] = small[0:rows, 64:128]
    gb_gate[...] = small[rows:, 0:piece]
    gb_up[...] = pltpu.roll(small[rows:, :], 64, 1)[:, 0:piece]


def on_device(
    acts, cot_hidden, gate_pre, up_pre, w_gate, w_up, gate_down_factor, up_down_factor, b_gate, b_up
):
    group_tok, width = acts.shape
    own_tok, hid = cot_hidden.shape
    n_chunk = own_tok // CHUNK
    dma = pltpu.SemaphoreType.DMA
    vmem = pltpu.VMEM
    shapes = (
        jax.ShapeDtypeStruct((group_tok // NZ, width), BF16),
        jax.ShapeDtypeStruct((width // 32, 64), F32),
        jax.ShapeDtypeStruct((width // 32, 64), F32),
        jax.ShapeDtypeStruct((64, hid // 32), F32),
        jax.ShapeDtypeStruct((64, hid // 32), F32),
    )
    results = pl.pallas_call(
        kernel,
        out_shape=(shapes[0], jax.ShapeDtypeStruct((width // 32 + 64, 128), F32)),
        in_specs=[pl.BlockSpec(memory_space=pl.ANY)] * 10,
        out_specs=(pl.BlockSpec(memory_space=pltpu.VMEM),) * 2,
        scratch_shapes=[
            vmem((3, own_tok, hid), BF16),
            vmem((width, 2 * hid), BF16),
            vmem((2 * hid, width), BF16),
            vmem((128, 2 * hid), BF16),
            vmem((128, width), BF16),
            vmem((own_tok, width), BF16),
            vmem((group_tok, width // NZ), BF16),
            vmem((n_chunk, NY, 2, CHUNK, 2 * hid), BF16),
            vmem((n_chunk, ROWS, CHUNK, width), F32),
            vmem((n_chunk, ROWS, CHUNK, width), BF16),
            vmem((n_chunk, 6, CHUNK, width), BF16),
            vmem((n_chunk, 2, CHUNK, width // 2), BF16),
            vmem((own_tok, width), F32),
            vmem((NZ, own_tok, 128), BF16),
            vmem((NY, 2, own_tok, 128), BF16),
            vmem((own_tok, 128), F32),
            vmem((own_tok // 2, 128), F32),
            vmem((own_tok // 2, 128), BF16),
            vmem((NY - 1, own_tok // 2, 128), BF16),
            vmem((NZ, own_tok, 128), BF16),
            vmem((NX, width // 32, 128), F32),
            vmem((NX - 1, width // 32, 128), F32),
            vmem((NX, 64, 128), F32),
            vmem((NX - 1, 64, 128), F32),
            dma((11,)),
            dma((n_chunk, 6, 2)),
            dma((2,)),
            dma((n_chunk, NY - 1, 2)),
            dma((n_chunk, 8, 2)),
            dma((NZ - 1, 2)),
            dma((NY - 1, 2)),
            dma((2,)),
            dma((2,)),
            dma((NY - 1, 2)),
            dma((NZ - 1, 2)),
            dma((2,)),
            dma((NX - 1, 2)),
            dma((NX - 1, 2)),
        ],
        compiler_params=pltpu.CompilerParams(
            collective_id=0, has_side_effects=True, vmem_limit_bytes=60 * 1024 * 1024
        ),
    )(
        acts,
        cot_hidden,
        gate_pre,
        up_pre,
        w_gate,
        w_up,
        gate_down_factor.T,
        up_down_factor.T,
        b_gate,
        b_up,
    )
    return pl.pallas_call(
        place,
        out_shape=shapes,
        in_specs=[pl.BlockSpec(memory_space=pltpu.VMEM)] * 2,
        out_specs=(pl.BlockSpec(memory_space=pltpu.VMEM),) * 5,
    )(*results)


def solution(mesh):
    in_specs = (
        P("dp", "row"),
        P(("dp", "row"), "col"),
        P(("dp", "row"), "col"),
        P(("dp", "row"), "col"),
        P("row", "col"),
        P("row", "col"),
        P(),
        P(),
        P(None, "col"),
        P(None, "col"),
    )
    out_specs = (
        P(("dp", "col"), "row"),
        P(("row", "col", "dp"), None),
        P(("row", "col", "dp"), None),
        P(None, ("col", "row", "dp")),
        P(None, ("col", "row", "dp")),
    )
    return jax.shard_map(
        on_device, mesh=mesh, in_specs=in_specs, out_specs=out_specs, check_vma=False
    )
```

```python
import jax
import jax.numpy as jnp
from jax import lax
from jax.experimental import pallas as pl
from jax.experimental.pallas import tpu as pltpu
from jax.sharding import PartitionSpec as P

MESH = pl.DeviceIdType.MESH
F32, BF16 = jnp.float32, jnp.bfloat16
ADAPTER_SCALE = 2.0
NY, NZ, NX = 4, 8, 4
ROWS = 2 * NY
CHUNK = 16


def times_transposed(left, right):
    return lax.dot_general(
        left, right, (((1,), (1,)), ((), ())), preferred_element_type=F32
    )


def kernel(
    acts,
    cot,
    gate_pre,
    up_pre,
    w_gate,
    w_up,
    gate_factor,
    up_factor,
    b_gate,
    b_up,
    out,
    small,
    pre,
    w,
    wt,
    b,
    fac,
    act_rows,
    act_cols,
    d,
    part,
    part_send,
    part_recv,
    half_recv,
    adapter,
    rank_part,
    rank_all,
    low_part,
    low_pair,
    low_chip,
    low_recv,
    low_all,
    ga_send,
    ga_recv,
    gb_send,
    gb_recv,
    in_sem,
    y_sem,
    po_sem,
    p_sem,
    z_sem,
    rz_sem,
    ry_sem,
    rp_sem,
    lp_sem,
    ly_sem,
    lz_sem,
    lq_sem,
    ga_sem,
    gb_sem,
):
    own_tok, hid = cot.shape
    group_tok, width = acts.shape
    n_chunk = own_tok // CHUNK
    factor = 2.0 / (group_tok * NX)
    r, c, x = lax.axis_index("row"), lax.axis_index("col"), lax.axis_index("dp")
    y, core = r // 2, r % 2
    sub = width // NZ
    half_tok = own_tok // 2
    near_half = pl.ds(pl.multiple_of(core * half_tok, half_tok), half_tok)
    far_half = pl.ds(pl.multiple_of((1 - core) * half_tok, half_tok), half_tok)

    width_at = pl.multiple_of(r * width, width)
    loads = [
        (cot, pre.at[0]),
        (gate_pre, pre.at[1]),
        (up_pre, pre.at[2]),
        (b_gate, b.at[0:64, 0:hid]),
        (b_up, b.at[64:128, hid : 2 * hid]),
        (acts.at[pl.ds(pl.multiple_of(c * own_tok, own_tok), own_tok), :], act_rows),
        (gate_factor.at[:, pl.ds(width_at, width)], fac.at[0:64]),
        (up_factor.at[:, pl.ds(width_at, width)], fac.at[64:128]),
        (w_gate, w.at[:, 0:hid]),
        (w_up, w.at[:, hid : 2 * hid]),
        (acts.at[:, pl.ds(pl.multiple_of(c * sub, sub), sub)], act_cols),
    ]
    loads = [pltpu.make_async_copy(src, dst, in_sem.at[i]) for i, (src, dst) in enumerate(loads)]
    for load in loads[0:8]:
        load.start()

    y_peer = [None] + [{"row": ((y + step) % NY) * 2 + core} for step in range(1, NY)]
    z_peer = [None] + [{"col": (c + step) % NZ} for step in range(1, NZ)]
    x_peer = [None] + [{"dp": (x + step) % NX} for step in range(1, NX)]
    partner = {"row": y * 2 + (1 - core)}
    peers = [partner] + y_peer[1:] + z_peer[1:] + x_peer[1:]
    barrier = pltpu.get_barrier_semaphore()
    for peer in peers:
        pl.semaphore_signal(barrier, 1, device_id=peer, device_id_type=MESH)

    sent = []

    def remote(src, dst, sem, where):
        return pltpu.make_async_remote_copy(
            src_ref=src,
            dst_ref=dst,
            send_sem=sem.at[0],
            recv_sem=sem.at[1],
            device_id=where,
            device_id_type=MESH,
        )

    def start(copy):
        copy.start()
        sent.append(copy)

    def cotangents(q):
        rows = slice(q * CHUNK, (q + 1) * CHUNK)
        gate = pre[1, rows, :].astype(F32)
        sig = jax.nn.sigmoid(gate)
        hot = pre[0, rows, :].astype(F32)
        up = pre[2, rows, :].astype(F32)
        d[q, y, core, :, 0:hid] = (hot * up * sig * (1.0 + gate * (1.0 - sig))).astype(BF16)
        d[q, y, core, :, hid : 2 * hid] = (hot * gate * sig).astype(BF16)

    right, left, far = (y + 1) % NY, (y + NY - 1) % NY, (y + 2) % NY

    def y_copy(q, kind):
        gate, up = slice(0, hid), slice(hid, 2 * hid)
        ref, step = (
            (d.at[q, y, core, :, gate], 1),
            (d.at[q, y, core, :, up], NY - 1),
            (d.at[q, y, core, :, up], 1),
            (d.at[q, y, core, :, gate], NY - 1),
            (d.at[q, left, core, :, gate], 1),
            (d.at[q, right, core, :, up], NY - 1),
        )[kind]
        return remote(ref, ref, y_sem.at[q, kind], y_peer[step])

    def p_own():
        ref = d.at[:, y, core]
        return remote(ref, ref, po_sem, partner)

    def p_copy(q, kind):
        ref = d.at[q, (left, right, far)[kind], core]
        return remote(ref, ref, p_sem.at[q, kind], partner)

    def own(q):
        for kind in range(4):
            start(y_copy(q, kind))

    def near(q):
        y_copy(q, 0).wait_recv()
        start(y_copy(q, 4))
        y_copy(q, 1).wait_recv()
        start(y_copy(q, 5))
        if q + 2 < n_chunk:
            own(q + 2)
        y_copy(q, 2).wait_recv()
        y_copy(q, 3).wait_recv()
        start(p_copy(q, 0))
        start(p_copy(q, 1))

    def far_in(q):
        y_copy(q, 4).wait_recv()
        y_copy(q, 5).wait_recv()
        start(p_copy(q, 2))

    def product(q):
        if q == 0:
            p_own().wait_recv()
        for kind in range(NY - 1):
            p_copy(q, kind).wait_recv()
        tile = jnp.dot(
            d[q].reshape(ROWS * CHUNK, 2 * hid), wt[...], preferred_element_type=F32
        ).reshape(ROWS, CHUNK, width)
        part[q] = tile
        part_send[q] = tile.astype(BF16)
        for kind in range(6):
            start(z_copy(q, kind))

    lower, upper = slice(0, width // 2), slice(width // 2, width)

    def z_copy(q, kind):
        sem = z_sem.at[q, kind]
        at = [(c + step) % NZ for step in range(NZ)]
        if kind == 0:
            return remote(part_send.at[q, at[4], :, lower], half_recv.at[q, 0], sem, z_peer[6])
        if kind == 1:
            return remote(part_send.at[q, at[4], :, upper], half_recv.at[q, 1], sem, z_peer[2])
        if kind == 2:
            return remote(part_send.at[q, at[5]], part_recv.at[q, 0], sem, z_peer[7])
        if kind == 3:
            return remote(part_send.at[q, at[3]], part_recv.at[q, 1], sem, z_peer[1])
        if kind == 4:
            return remote(part_send.at[q, at[7]], part_recv.at[q, 2], sem, z_peer[7])
        if kind == 5:
            return remote(part_send.at[q, at[1]], part_recv.at[q, 3], sem, z_peer[1])
        if kind == 6:
            return remote(part_send.at[q, at[6]], part_recv.at[q, 4], sem, z_peer[6])
        return remote(part_send.at[q, at[2]], part_recv.at[q, 5], sem, z_peer[2])

    def z_on(q):
        for side, (same, other, step) in enumerate(((lower, upper, 6), (upper, lower, 2))):
            at = (c + step) % NZ
            z_copy(q, 2 + side).wait_recv()
            z_copy(q, side).wait_recv()
            total = part[q, at, :, same] + part_recv[q, side, :, same].astype(F32)
            total = total + half_recv[q, side].astype(F32)
            part_send[q, at, :, same] = total.astype(BF16)
            total = part[q, at, :, other] + part_recv[q, side, :, other].astype(F32)
            part_send[q, at, :, other] = total.astype(BF16)
            start(z_copy(q, 6 + side))

    def z_last(q):
        rows = slice(q * CHUNK, (q + 1) * CHUNK)
        total = part[q, c] + adapter[rows, :]
        for kind in range(4, 8):
            z_copy(q, kind).wait_recv()
            total = total + part_recv[q, kind - 2].astype(F32)
        out[rows, :] = total.astype(BF16)

    def rank_z(step):
        ref = rank_part.at[c]
        return remote(ref, ref, rz_sem.at[step - 1], z_peer[step])

    def rank_y(step):
        ref = rank_all.at[y, core]
        return remote(ref, ref, ry_sem.at[step - 1], y_peer[step])

    def rank_p():
        ref = rank_all.at[:, core]
        return remote(ref, ref, rp_sem, partner)

    def low_p():
        return remote(low_part.at[far_half], low_pair, lp_sem, partner)

    def low_y(step):
        return remote(low_chip, low_recv.at[step - 1], ly_sem.at[step - 1], y_peer[step])

    def low_z(step):
        ref = low_all.at[c, near_half]
        return remote(ref, ref, lz_sem.at[step - 1], z_peer[step])

    def low_q():
        ref = low_all.at[:, near_half]
        return remote(ref, ref, lq_sem, partner)

    def ga_copy(step):
        return remote(
            ga_send.at[(x + step) % NX], ga_recv.at[step - 1], ga_sem.at[step - 1], x_peer[step]
        )

    def gb_copy(step):
        return remote(
            gb_send.at[(x + step) % NX], gb_recv.at[step - 1], gb_sem.at[step - 1], x_peer[step]
        )

    for load in loads[0:3]:
        load.wait()
    for load in loads[8:]:
        load.start()
    cotangents(0)
    pl.semaphore_wait(barrier, len(peers))
    own(0)
    cotangents(1)
    own(1)
    cotangents(2)
    cotangents(3)
    start(p_own())
    b[0:64, hid : 2 * hid] = jnp.zeros((64, hid), BF16)
    b[64:128, 0:hid] = jnp.zeros((64, hid), BF16)
    for load in loads[3:8]:
        load.wait()
    low_part[...] = times_transposed(act_rows[...], fac[...])
    start(low_p())
    rank_part[c] = times_transposed(d[:, y, core].reshape(own_tok, 2 * hid), b[...]).astype(BF16)
    for step in range(1, NZ):
        start(rank_z(step))

    low_p().wait_recv()
    low_own = low_part[near_half, :] + low_pair[...]
    low_chip[...] = low_own.astype(BF16)
    for step in range(1, NY):
        start(low_y(step))
    near(0)

    for load in loads[8:]:
        load.wait()

    @pl.loop(0, 2 * hid // 256)
    def _(n):
        at = pl.ds(pl.multiple_of(n * 256, 256), 256)
        wt[at, :] = w[:, at].T

    near(1)
    for step in range(1, NY):
        low_y(step).wait_recv()
        low_own = low_own + low_recv[step - 1].astype(F32)
    low_all[c, near_half] = low_own.astype(BF16)
    for step in range(1, NZ):
        start(low_z(step))
    far_in(0)
    product(0)
    total = rank_part[c].astype(F32)
    for step in range(1, NZ):
        rank_z(step).wait_recv()
        total = total + rank_part[(c + NZ - step) % NZ].astype(F32)
    rank_all[y, core] = total.astype(BF16)
    for step in range(1, NY):
        start(rank_y(step))
    near(2)
    far_in(1)
    product(1)
    z_on(0)
    near(3)
    far_in(2)
    product(2)
    z_on(1)
    far_in(3)
    for step in range(1, NY):
        rank_y(step).wait_recv()
    start(rank_p())
    for step in range(1, NZ):
        low_z(step).wait_recv()
    start(low_q())
    product(3)
    low_q().wait_recv()

    mine = hid // ROWS
    piece = mine // NX
    window = 384
    base = jnp.minimum((r * mine) // 128 * 128, hid - window)
    shift = r * mine - base
    gate_sum = jnp.zeros((64, window), F32)
    up_sum = jnp.zeros((64, window), F32)
    for q in range(n_chunk):
        low_t = low_all[:, q * CHUNK : (q + 1) * CHUNK, :].reshape(ROWS * CHUNK, 128).T
        at = pl.ds(pl.multiple_of(base, 128), window)
        gate_sum += jnp.dot(
            low_t[0:64],
            d[q, :, :, :, at].reshape(ROWS * CHUNK, window),
            preferred_element_type=F32,
        )
        at = pl.ds(pl.multiple_of(hid + base, 128), window)
        up_sum += jnp.dot(
            low_t[64:128],
            d[q, :, :, :, at].reshape(ROWS * CHUNK, window),
            preferred_element_type=F32,
        )
    gate_sum = factor * gate_sum
    up_sum = factor * up_sum
    lane = lax.broadcasted_iota(jnp.int32, (64, 128), 1)
    for e in range(NX):
        at = shift + e * piece
        gate_at = pltpu.roll(gate_sum, window - at, 1)[:, 0:128]
        up_at = pltpu.roll(up_sum, (window + 64 - at) % window, 1)[:, 0:128]
        gb_send[e] = jnp.where(lane < 64, gate_at, up_at)
    for step in range(1, NX):
        start(gb_copy(step))

    rank_p().wait_recv()
    total = factor * lax.dot_general(
        act_cols[...],
        rank_all[...].reshape(group_tok, 128),
        (((0,), (0,)), ((), ())),
        preferred_element_type=F32,
    )
    ga_send[...] = total.reshape(NX, sub // NX, 128)
    for step in range(1, NX):
        start(ga_copy(step))
    adapter[...] = ADAPTER_SCALE * jnp.dot(
        rank_all[c // 2, c % 2], fac[...], preferred_element_type=F32
    )

    z_on(2)
    z_last(0)
    z_last(1)
    z_on(3)
    total = gb_send[x]
    for step in range(1, NX):
        gb_copy(step).wait_recv()
        total = total + gb_recv[step - 1]
    small[sub // NX :, :] = total
    total = ga_send[x]
    for step in range(1, NX):
        ga_copy(step).wait_recv()
        total = total + ga_recv[step - 1]
    small[0 : sub // NX, :] = total
    z_last(2)
    z_last(3)
    for copy in sent:
        copy.wait_send()


def place(out_in, small, out, ga_gate, ga_up, gb_gate, gb_up):
    rows, piece = ga_gate.shape[0], gb_gate.shape[1]
    out[...] = out_in[...]
    ga_gate[...] = small[0:rows, 0:64]
    ga_up[...] = small[0:rows, 64:128]
    gb_gate[...] = small[rows:, 0:piece]
    gb_up[...] = pltpu.roll(small[rows:, :], 64, 1)[:, 0:piece]


def on_device(
    acts, cot_hidden, gate_pre, up_pre, w_gate, w_up, gate_down_factor, up_down_factor, b_gate, b_up
):
    group_tok, width = acts.shape
    own_tok, hid = cot_hidden.shape
    n_chunk = own_tok // CHUNK
    dma = pltpu.SemaphoreType.DMA
    vmem = pltpu.VMEM
    shapes = (
        jax.ShapeDtypeStruct((group_tok // NZ, width), BF16),
        jax.ShapeDtypeStruct((width // 32, 64), F32),
        jax.ShapeDtypeStruct((width // 32, 64), F32),
        jax.ShapeDtypeStruct((64, hid // 32), F32),
        jax.ShapeDtypeStruct((64, hid // 32), F32),
    )
    results = pl.pallas_call(
        kernel,
        out_shape=(shapes[0], jax.ShapeDtypeStruct((width // 32 + 64, 128), F32)),
        in_specs=[pl.BlockSpec(memory_space=pl.ANY)] * 10,
        out_specs=(pl.BlockSpec(memory_space=pltpu.VMEM),) * 2,
        scratch_shapes=[
            vmem((3, own_tok, hid), BF16),
            vmem((width, 2 * hid), BF16),
            vmem((2 * hid, width), BF16),
            vmem((128, 2 * hid), BF16),
            vmem((128, width), BF16),
            vmem((own_tok, width), BF16),
            vmem((group_tok, width // NZ), BF16),
            vmem((n_chunk, NY, 2, CHUNK, 2 * hid), BF16),
            vmem((n_chunk, ROWS, CHUNK, width), F32),
            vmem((n_chunk, ROWS, CHUNK, width), BF16),
            vmem((n_chunk, 6, CHUNK, width), BF16),
            vmem((n_chunk, 2, CHUNK, width // 2), BF16),
            vmem((own_tok, width), F32),
            vmem((NZ, own_tok, 128), BF16),
            vmem((NY, 2, own_tok, 128), BF16),
            vmem((own_tok, 128), F32),
            vmem((own_tok // 2, 128), F32),
            vmem((own_tok // 2, 128), BF16),
            vmem((NY - 1, own_tok // 2, 128), BF16),
            vmem((NZ, own_tok, 128), BF16),
            vmem((NX, width // 32, 128), F32),
            vmem((NX - 1, width // 32, 128), F32),
            vmem((NX, 64, 128), F32),
            vmem((NX - 1, 64, 128), F32),
            dma((11,)),
            dma((n_chunk, 6, 2)),
            dma((2,)),
            dma((n_chunk, NY - 1, 2)),
            dma((n_chunk, 8, 2)),
            dma((NZ - 1, 2)),
            dma((NY - 1, 2)),
            dma((2,)),
            dma((2,)),
            dma((NY - 1, 2)),
            dma((NZ - 1, 2)),
            dma((2,)),
            dma((NX - 1, 2)),
            dma((NX - 1, 2)),
        ],
        compiler_params=pltpu.CompilerParams(
            collective_id=0, has_side_effects=True, vmem_limit_bytes=60 * 1024 * 1024
        ),
    )(
        acts,
        cot_hidden,
        gate_pre,
        up_pre,
        w_gate,
        w_up,
        gate_down_factor.T,
        up_down_factor.T,
        b_gate,
        b_up,
    )
    return pl.pallas_call(
        place,
        out_shape=shapes,
        in_specs=[pl.BlockSpec(memory_space=pltpu.VMEM)] * 2,
        out_specs=(pl.BlockSpec(memory_space=pltpu.VMEM),) * 5,
    )(*results)


def solution(mesh):
    in_specs = (
        P("dp", "row"),
        P(("dp", "row"), "col"),
        P(("dp", "row"), "col"),
        P(("dp", "row"), "col"),
        P("row", "col"),
        P("row", "col"),
        P(),
        P(),
        P(None, "col"),
        P(None, "col"),
    )
    out_specs = (
        P(("dp", "col"), "row"),
        P(("row", "col", "dp"), None),
        P(("row", "col", "dp"), None),
        P(None, ("col", "row", "dp")),
        P(None, ("col", "row", "dp")),
    )
    return jax.shard_map(
        on_device, mesh=mesh, in_specs=in_specs, out_specs=out_specs, check_vma=False
    )
```
